256 devices in a mesh: sub: 32 (over z, y), top: 8 (over x, core).
Axes of the slice: x: 4, y: 4, z: 8, core: 2. Of those that a mesh axis runs over, the one named last changes fastest.
Arguments:
- coords: float32 [3, 1048576], P(None, ('top', 'sub')), may hold values from 0 to 1, as said below
- vectors: float32 [1048576, 128], P(('top', 'sub')), may hold values from -6 to 6
- order: int32 [256, 4096], P(('top', 'sub')), may hold values from 0 to 4095, each once within a row
- generators: bfloat16 [1048576, 128], P(('top', 'sub')), may hold values from -0.125 to 0.125
- leaf_transfer: bfloat16 [512, 128, 128], P(('top', 'sub')), may hold values from -0.375 to 0.375
- leaf_coupling: bfloat16 [256, 128, 128], P(('top', 'sub')), may hold values from -0.5 to 0.5
- sub_transfer: bfloat16 [8, 62, 128, 128], P('top'), may hold values from -0.375 to 0.375
- sub_coupling: bfloat16 [8, 31, 128, 128], P('top'), may hold values from -0.5 to 0.5
- top_transfer: bfloat16 [12, 128, 128], replicated, may hold values from -0.375 to 0.375
- top_coupling: bfloat16 [7, 128, 128], replicated, may hold values from -0.5 to 0.5
Outputs:
- product: float32 [1048576, 128], P(('top', 'sub'))
The draws below stay inside these ranges and needn't reach their ends.
Inputs may be any that keep to these rules, and one draw needn't show every extreme that they name: Each row of order is a permutation of 0 to 4095. `coords`: coordinates lie in the unit cube.
All inputs are finite; a program needn't handle non-finite values.
Results may differ from the reference program's by a relative error of at most 0.0035.
Values sent between devices are 32-bit elements; how exact they have to be, the bound alone decides.
A program may use at most 64 MiB of HBM per device.

```python
import jax
import jax.numpy as jnp
from jax import lax

R = 128
C = 128
LEAF = 2048
LEAVES_DEV = 2
ROWS_DEV = 4096
POINTS = 1048576
LEAVES = 512
N_SUB = 32
N_TOP = 8
DEVICES = 256


def draw_coords(key, part):
    key = jax.random.fold_in(key, 11)
    centre_key, inner_key = jax.random.split(key)
    side_length = 0.08
    centres = jax.random.uniform(centre_key, (3, LEAVES, 1), jnp.float32, 0.0, 1.0 - side_length)
    unit_inside = jax.random.uniform(inner_key, (3, LEAVES, LEAF), jnp.float32, 0.0, 1.0)
    return (centres + side_length * unit_inside).reshape(3, LEAVES * LEAF)


def block_levels(key, shape, cuts, low, top_value):
    factor_of, own = 1.0, jax.random.fold_in(key, 6)
    for axis_at, shards_of in cuts:
        steps = jnp.exp(jax.random.uniform(jax.random.fold_in(own, axis_at), (shards_of,), jnp.float32, low / len(cuts), top_value / len(cuts)))
        factor_of = factor_of * jnp.repeat(steps, shape[axis_at] // shards_of).reshape([-1 if axis == axis_at else 1 for axis in range(len(shape))])
    return factor_of


def normal_values(key, extent, spread, limit, shards=(), dtype=jnp.bfloat16):
    values = jax.random.normal(key, extent, jnp.float32) * spread
    if len(shards) > 0:
        values = block_levels(key, extent, shards, -0.22, 0.18) * values
    return jnp.clip(values, min=-limit, max=limit).astype(dtype)


def setup_inputs(seed: int = 0) -> dict:
    arg_keys = jax.random.split(jax.random.key(seed), 11)
    return {
        "coords": draw_coords(jax.random.fold_in(arg_keys[10], 71), 0),
        "vectors": normal_values(arg_keys[1], (POINTS, C), 1.0, 6.0, ((0, 256),), jnp.float32),
        "order": jax.vmap(lambda own: jax.random.permutation(own, ROWS_DEV))(jax.random.split(arg_keys[2], DEVICES)).reshape((DEVICES, ROWS_DEV)).astype(jnp.int32),
        "generators": normal_values(arg_keys[3], (POINTS, R), LEAF ** -0.5, 0.125, ((0, 256),)),
        "leaf_transfer": normal_values(arg_keys[4], (LEAVES, R, R), (2 * R) ** -0.5, 0.375, ((0, 256),)),
        "leaf_coupling": normal_values(arg_keys[5], (DEVICES, R, R), R ** -0.5, 0.5, ((0, 256),)),
        "sub_transfer": normal_values(arg_keys[6], (N_TOP, 2 * N_SUB - 2, R, R), (2 * R) ** -0.5, 0.375, ((0, 8),)),
        "sub_coupling": normal_values(arg_keys[7], (N_TOP, N_SUB - 1, R, R), R ** -0.5, 0.5, ((0, 8),)),
        "top_transfer": normal_values(arg_keys[8], (2 * N_TOP - 4, R, R), (2 * R) ** -0.5, 0.375),
        "top_coupling": normal_values(arg_keys[9], (N_TOP - 1, R, R), R ** -0.5, 0.5),
    }


PRECISE = lax.Precision.HIGHEST
NUGGET = 0.1
DECAY_RATE = 3.0 ** 0.5 / 0.004

def lift_coeffs(transfer, coeffs):
    return jnp.dot(transfer.astype(jnp.float32).T, coeffs, precision=PRECISE)

def push_field(transfer, field_now):
    return jnp.dot(transfer.astype(jnp.float32), field_now, precision=PRECISE)

def couple_left(couple, coeffs):
    return jnp.dot(couple.astype(jnp.float32), coeffs, precision=PRECISE)

def couple_right(couple, coeffs):
    return jnp.dot(couple.astype(jnp.float32).T, coeffs, precision=PRECISE)

def level_up(coeffs, transfer, couple):
    portion = jax.vmap(lift_coeffs)(transfer, coeffs)
    left_terms = jax.vmap(couple_left)(couple, coeffs[1::2])
    right_terms = jax.vmap(couple_right)(couple, coeffs[0::2])
    sibling_terms = jnp.stack([left_terms, right_terms], axis=1).reshape(coeffs.shape)
    return (portion[0::2] + portion[1::2], sibling_terms)

def leaf_coeffs(gen_rows, rounded):
    return lax.dot_general(gen_rows, rounded, (((0,), (0,)), ((), ())), preferred_element_type=jnp.float32)

def leaf_apply(packed):
    points, rounded, ordered, gen_rows, leaf_field = packed
    leaf_size = points.shape[1]
    block_size = min(512, leaf_size)
    row_points = points.reshape(3, leaf_size // block_size, block_size).transpose(1, 0, 2)

    def nearby(block_points):
        offset = block_points[:, :, None] - points[:, None, :]
        radius = jnp.sqrt(lax.optimization_barrier(jnp.sum(offset * offset, axis=0)))
        kernel = ((1.0 + DECAY_RATE * radius) * jnp.exp(-DECAY_RATE * radius)).astype(jnp.bfloat16)
        return jnp.dot(kernel, rounded, preferred_element_type=jnp.float32)
    direct = lax.map(nearby, row_points).reshape(leaf_size, rounded.shape[1])
    far_part = jnp.dot(gen_rows, leaf_field.astype(jnp.bfloat16), preferred_element_type=jnp.float32)
    return direct + far_part + NUGGET * ordered

def permute_rows(block_rows, positions):
    return block_rows[positions]

def restore_rows(block_rows, positions):
    return jnp.zeros_like(block_rows).at[positions].set(block_rows)

def reference(coords, vectors, order, generators, leaf_transfer, leaf_coupling, sub_transfer, sub_coupling, top_transfer, top_coupling):
    leaf_count = DEVICES * LEAVES_DEV
    blocks = vectors.reshape(DEVICES, ROWS_DEV, C)
    ordered = jax.vmap(permute_rows)(blocks, order).reshape(leaf_count, LEAF, C)
    rounded = ordered.astype(jnp.bfloat16)
    gen_rows = generators.reshape(leaf_count, LEAF, R)
    coeffs = jax.vmap(leaf_coeffs)(gen_rows, rounded)
    levels = [(leaf_transfer, leaf_coupling)]
    node_count = N_SUB
    while node_count > 1:
        levels.append((sub_transfer[:, node_count - 2:2 * node_count - 2].reshape(-1, R, R), sub_coupling[:, node_count // 2 - 1:node_count - 1].reshape(-1, R, R)))
        node_count //= 2
    node_count = N_TOP
    while node_count > 1:
        if node_count >= 4:
            transfer = top_transfer[node_count - 4:2 * node_count - 4]
        else:
            transfer = jnp.zeros((node_count, R, R), jnp.bfloat16)
        levels.append((transfer, top_coupling[node_count // 2 - 1:node_count - 1]))
        node_count //= 2
    sibling_list = []
    for transfer, couple in levels:
        coeffs, sibling_terms = level_up(coeffs, transfer, couple)
        sibling_list.append(sibling_terms)
    field_now = jnp.zeros((1, R, C), jnp.float32)
    for level_pair, sibling_terms in zip(levels[::-1], sibling_list[::-1]):
        field_now = jax.vmap(push_field)(level_pair[0], jnp.repeat(field_now, 2, axis=0)) + sibling_terms
    points = coords.reshape(3, leaf_count, LEAF).transpose(1, 0, 2)
    nearby_rows = lax.map(leaf_apply, (points, rounded, ordered, gen_rows, field_now))
    nearby_rows = nearby_rows.reshape(DEVICES, ROWS_DEV, C)
    result = jax.vmap(restore_rows)(nearby_rows, order)
    return result.reshape(DEVICES * ROWS_DEV, C)
```

```python
import functools

import jax
import jax.numpy as jnp
from jax import lax
from jax.experimental import pallas as pl
from jax.experimental.pallas import tpu as pltpu
from jax.sharding import PartitionSpec as P

NUGGET = 0.1
DECAY_RATE = 3.0**0.5 / 0.004
TINY = 1e-30
BLOCK = 256
BLOCKS = 8
WIDE = 5 * BLOCK
NARROW = 4 * BLOCK
F32 = jnp.float32
BF16 = jnp.bfloat16
NN = (((1,), (0,)), ((), ()))
NT = (((1,), (1,)), ((), ()))


def pieces(x):
    high = x.astype(BF16)
    low = (x - high.astype(F32)).astype(BF16)
    return jnp.concatenate([high, low], axis=0)


def product(x, matrix, form):
    rows = x.shape[0]
    both = lax.dot_general(pieces(x), matrix, form, preferred_element_type=F32)
    return both[:rows] + both[rows:]


def main_kernel(
    n_sub,
    n_top,
    order_ref,
    coords_ref,
    vectors_hbm,
    gen_hbm,
    leaf_w_hbm,
    leaf_b_hbm,
    sub_w_hbm,
    sub_b_hbm,
    top_w_hbm,
    top_b_hbm,
    y_hbm,
    vec,
    ordered,
    v_ext,
    v_t,
    gen,
    leaf_w,
    leaf_b,
    sub_w,
    sub_b,
    top_w,
    top_b,
    x_rows,
    x_cols,
    k_buf,
    y_row,
    y_col,
    send_c,
    coef,
    sib,
    field,
    send_f,
    back,
    top_c,
    dev_f,
    g_leaf,
    y_out,
    in_sem,
    out_sem,
    own_sem,
    send_sem,
    recv_sem,
):
    leaf = v_t.shape[2]
    rows = vec.shape[0]
    width = vec.shape[1]
    share = width // n_sub
    me_sub = lax.axis_index("sub")
    me_top = lax.axis_index("top")

    barrier = pltpu.get_barrier_semaphore()

    def greet(axis, count, place):
        def one(k, _):
            pl.semaphore_signal(
                barrier,
                inc=1,
                device_id={axis: lax.rem(place + k, count)},
                device_id_type=pl.DeviceIdType.MESH,
            )
            return 0

        lax.fori_loop(1, count, one, 0)

    loads = [
        pltpu.make_async_copy(source, target, in_sem.at[i])
        for i, (source, target) in enumerate(
            [
                (vectors_hbm, vec),
                (gen_hbm, gen),
                (leaf_w_hbm, leaf_w),
                (leaf_b_hbm, leaf_b),
                (sub_w_hbm, sub_w),
                (sub_b_hbm, sub_b),
                (top_w_hbm, top_w),
                (top_b_hbm, top_b),
            ]
        )
    ]
    for load in loads:
        load.start()
    greet("sub", n_sub, me_sub)
    greet("top", n_top, me_top)

    def spread(block, _):
        start = pl.multiple_of(block * 128, 128)
        for axis in range(3):
            row = coords_ref[axis : axis + 1, pl.ds(start, 128)] * DECAY_RATE
            x_rows[axis, pl.ds(start, 128), :] = jnp.broadcast_to(row, (128, 128)).T
        return 0

    lax.fori_loop(0, rows // 128, spread, 0)
    extra = v_ext.shape[1] - leaf
    for at in range(2):
        for axis in range(3):
            row = coords_ref[axis : axis + 1, at * leaf : (at + 1) * leaf] * DECAY_RATE
            whole = jnp.broadcast_to(row, (8, leaf))
            x_cols[axis, at, :, :leaf] = whole
            x_cols[axis, at, :, leaf:] = whole[:, :extra]
    y_col[...] = jnp.zeros_like(y_col)

    loads[0].wait()

    def move(group, _):
        base = pl.multiple_of(group * 16, 16)
        for k in range(16):
            ordered[pl.ds(base + k, 1), :] = vec[pl.ds(order_ref[0, base + k], 1), :]
        return 0

    lax.fori_loop(0, rows // 16, move, 0)
    for at in range(2):

        def turn(block, _):
            start = pl.multiple_of(block * 128, 128)
            part = ordered[pl.ds(at * leaf + start, 128), :]
            v_ext[at, pl.ds(start, 128), :] = part.astype(BF16)
            v_t[at, :, pl.ds(start, 128)] = part.T.astype(BF16)
            return 0

        lax.fori_loop(0, leaf // 128, turn, 0)
        v_ext[at, leaf:, :] = v_ext[at, :extra, :]

    for load in loads[1:4]:
        load.wait()
    left = jnp.dot(v_t[0], gen[:leaf, :], preferred_element_type=F32)
    right = jnp.dot(v_t[1], gen[leaf:, :], preferred_element_type=F32)
    device_c = product(left, leaf_w[0], NN) + product(right, leaf_w[1], NN)
    for r in range(n_sub):
        send_c[r] = device_c[r * share : (r + 1) * share, :]
    pl.semaphore_wait(barrier, n_sub + n_top - 2)

    def exchange(axis, count, place, stage, source, target, base):
        def copy(partner, slot):
            return pltpu.make_async_remote_copy(
                src_ref=source(partner),
                dst_ref=target.at[base + slot],
                send_sem=send_sem.at[stage, partner],
                recv_sem=recv_sem.at[stage, slot],
                device_id={axis: partner},
                device_id_type=pl.DeviceIdType.MESH,
            )

        def start(k, _):
            copy(lax.rem(place + k, count), place).start()
            return 0

        def finish_send(k, _):
            copy(lax.rem(place + k, count), place).wait_send()
            return 0

        def finish_recv(k, _):
            partner = lax.rem(place + k, count)
            copy(partner, partner).wait_recv()
            return 0

        return (
            lambda: lax.fori_loop(1, count, start, 0),
            lambda: lax.fori_loop(1, count, finish_send, 0),
            lambda: lax.fori_loop(1, count, finish_recv, 0),
        )

    up_start, up_sent, up_here = exchange(
        "sub", n_sub, me_sub, 0, lambda partner: send_c.at[partner], coef, n_sub
    )
    up_start()
    coef[n_sub + me_sub] = send_c[me_sub]
    g_leaf[0] = product(right, leaf_b[0], NT)
    g_leaf[1] = product(left, leaf_b[0], NN)

    def evaluate(at, block, size):
        def some_rows(part, _):
            first = part * 32
            here = pl.ds(pl.multiple_of(at * leaf + block * BLOCK + first, 32), 32)
            x_i = [x_rows[axis, here, :] for axis in range(3)]
            x_i = [jnp.concatenate([x, x], axis=1) for x in x_i]
            for step in range(size // BLOCK):
                there = pl.ds(pl.multiple_of((block + step) * BLOCK, BLOCK), BLOCK)
                total = None
                for axis in range(3):
                    x_j = x_cols[axis, at, :, there]
                    offset = x_i[axis] - jnp.concatenate([x_j] * 4, axis=0)
                    square = offset * offset
                    total = square + TINY if total is None else total + square
                scaled = total * lax.rsqrt(total)
                value = (1.0 + scaled) * jnp.exp(-scaled)
                k_buf[at, pl.ds(first, 32), pl.ds(step * BLOCK, BLOCK)] = value.astype(BF16)
            return 0

        lax.fori_loop(0, BLOCK // 32, some_rows, 0, unroll=True)

    def apply(at, block, size):
        start = pl.multiple_of(block * BLOCK, BLOCK)
        after = pl.multiple_of((block + 1) * BLOCK, BLOCK)
        y_row[at, pl.ds(start, BLOCK), :] = jnp.dot(
            k_buf[at, :, :size], v_ext[at, pl.ds(start, size), :], preferred_element_type=F32
        )
        y_col[at, :, pl.ds(after, size - BLOCK)] += jnp.dot(
            v_t[at, :, pl.ds(start, BLOCK)], k_buf[at, :, BLOCK:size], preferred_element_type=F32
        )

    def near(first, last, size):
        evaluate(0, first, size)
        apply(0, first, size)
        evaluate(1, first, size)

        def step(block, _):
            evaluate(0, block, size)
            apply(1, block - 1, size)
            evaluate(1, block, size)
            apply(0, block, size)
            return 0

        lax.fori_loop(first + 1, last, step, 0)
        apply(1, last - 1, size)

    near(0, 2, WIDE)

    loads[4].wait()
    loads[5].wait()
    up_here()

    def upward(held, matrices, parent, offset):
        pair = jnp.concatenate([held[2 * parent], held[2 * parent + 1]], axis=1)
        both = matrices[pl.ds(2 * parent - offset, 2)].reshape(2 * width, width)
        held[parent] = product(pair, both, NN)

    count = n_sub // 2
    while count >= 1:
        lax.fori_loop(
            count, 2 * count, lambda p, _: (upward(coef, sub_w, p, 2), 0)[1], 0, unroll=True
        )
        count //= 2
    top_start, top_sent, top_here = exchange(
        "top", n_top, me_top, 1, lambda partner: coef.at[1], top_c, n_top
    )
    top_start()
    top_c[n_top + me_top] = coef[1]

    def siblings(parent, _):
        matrix = sub_b[parent - 1]
        sib[2 * parent] = product(coef[2 * parent + 1], matrix, NT)
        sib[2 * parent + 1] = product(coef[2 * parent], matrix, NN)
        return 0

    lax.fori_loop(1, n_sub, siblings, 0, unroll=True)

    near(2, 4, WIDE)

    loads[6].wait()
    loads[7].wait()
    top_here()
    count = n_top // 2
    while count >= 2:
        lax.fori_loop(
            count, 2 * count, lambda p, _: (upward(top_c, top_w, p, 4), 0)[1], 0, unroll=True
        )
        count //= 2
    now = None
    count = 2
    while count <= n_top:
        node = count + me_top // (n_top // count)
        parent = node // 2
        is_left = node - 2 * parent == 0
        other = jnp.where(is_left, node + 1, node - 1)
        matrix = top_b[parent - 1]
        incoming = jnp.where(
            is_left, product(top_c[other], matrix, NT), product(top_c[other], matrix, NN)
        )
        now = incoming if now is None else product(now, top_w[node - 4], NT) + incoming
        count *= 2
    field[1] = now

    def downward(parent, _):
        both = sub_w[pl.ds(2 * parent - 2, 2)].reshape(2 * width, width)
        down = product(field[parent], both, NT)
        field[2 * parent] = down[:, :width] + sib[2 * parent]
        field[2 * parent + 1] = down[:, width:] + sib[2 * parent + 1]
        return 0

    count = 1
    while count < n_sub:
        lax.fori_loop(count, 2 * count, downward, 0, unroll=True)
        count *= 2
    down_start, down_sent, down_here = exchange(
        "sub", n_sub, me_sub, 2, lambda partner: field.at[n_sub + partner], back, 0
    )
    down_start()
    back[me_sub] = field[n_sub + me_sub]

    near(4, 8, NARROW)

    down_here()
    for r in range(n_sub):
        dev_f[r * share : (r + 1) * share, :] = back[r]
    device_f = dev_f[...]
    leaf_f = [
        (product(device_f, leaf_w[at], NT) + g_leaf[at]).astype(BF16) for at in range(2)
    ]

    writes = []
    for at in range(2):
        for block in range(BLOCKS):
            start = at * leaf + block * BLOCK
            here = slice(block * BLOCK, (block + 1) * BLOCK)
            turned = y_col[at, :, here]
            if (block + 1) * BLOCK <= extra:
                turned = turned + y_col[at, :, leaf + block * BLOCK : leaf + (block + 1) * BLOCK]
            far = lax.dot_general(
                gen[start : start + BLOCK, :], leaf_f[at], NT, preferred_element_type=F32
            )
            y_out[start : start + BLOCK, :] = (
                y_row[at, here, :] + turned.T + far + NUGGET * ordered[start : start + BLOCK, :]
            )
        half = pl.ds(at * leaf, leaf)
        write = pltpu.make_async_copy(y_out.at[half], y_hbm.at[half], out_sem.at[at])
        write.start()
        writes.append(write)
    up_sent()
    top_sent()
    down_sent()
    for write in writes:
        write.wait()


def scatter_kernel(order_ref, y_ref, out_ref):
    chunk = y_ref.shape[0]
    first = pl.program_id(0) * chunk

    def move(group, _):
        base = pl.multiple_of(group * 16, 16)
        for k in range(16):
            out_ref[pl.ds(order_ref[0, first + base + k], 1), :] = y_ref[pl.ds(base + k, 1), :]
        return 0

    lax.fori_loop(0, chunk // 16, move, 0)


def local(
    n_sub,
    n_top,
    coords,
    vectors,
    order,
    generators,
    leaf_transfer,
    leaf_coupling,
    sub_transfer,
    sub_coupling,
    top_transfer,
    top_coupling,
):
    rows, width = vectors.shape
    leaf = rows // 2
    rank = generators.shape[1]
    share = width // n_sub
    extended = leaf + 3 * BLOCK
    smem = pl.BlockSpec(memory_space=pltpu.SMEM)
    vmem = pl.BlockSpec(memory_space=pltpu.VMEM)
    hbm = pl.BlockSpec(memory_space=pl.ANY)
    scratch = [
        pltpu.VMEM((rows, width), F32),
        pltpu.VMEM((rows, width), F32),
        pltpu.VMEM((2, extended, width), BF16),
        pltpu.VMEM((2, width, leaf), BF16),
        pltpu.VMEM((rows, rank), BF16),
        pltpu.VMEM(leaf_transfer.shape, BF16),
        pltpu.VMEM(leaf_coupling.shape, BF16),
        pltpu.VMEM(sub_transfer.shape[1:], BF16),
        pltpu.VMEM(sub_coupling.shape[1:], BF16),
        pltpu.VMEM(top_transfer.shape, BF16),
        pltpu.VMEM(top_coupling.shape, BF16),
        pltpu.VMEM((3, rows, 128), F32),
        pltpu.VMEM((3, 2, 8, extended), F32),
        pltpu.VMEM((2, BLOCK, WIDE), BF16),
        pltpu.VMEM((2, leaf, width), F32),
        pltpu.VMEM((2, width, extended), F32),
        pltpu.VMEM((n_sub, share, rank), F32),
        pltpu.VMEM((2 * n_sub, share, rank), F32),
        pltpu.VMEM((2 * n_sub, share, rank), F32),
        pltpu.VMEM((2 * n_sub, share, rank), F32),
        pltpu.VMEM((n_sub, share, rank), F32),
        pltpu.VMEM((n_sub, share, rank), F32),
        pltpu.VMEM((2 * n_top, share, rank), F32),
        pltpu.VMEM((width, rank), F32),
        pltpu.VMEM((2, width, rank), F32),
        pltpu.VMEM((rows, width), F32),
        pltpu.SemaphoreType.DMA((8,)),
        pltpu.SemaphoreType.DMA((2,)),
        pltpu.SemaphoreType.DMA,
        pltpu.SemaphoreType.DMA((3, max(n_sub, n_top))),
        pltpu.SemaphoreType.DMA((3, max(n_sub, n_top))),
    ]
    y = pl.pallas_call(
        functools.partial(main_kernel, n_sub, n_top),
        out_shape=jax.ShapeDtypeStruct((rows, width), F32),
        in_specs=[smem, vmem] + [hbm] * 8,
        out_specs=hbm,
        scratch_shapes=scratch,
        compiler_params=pltpu.CompilerParams(
            collective_id=0, has_side_effects=True, vmem_limit_bytes=48 * 1024 * 1024
        ),
        name="hss_main",
    )(
        order,
        coords,
        vectors,
        generators,
        leaf_transfer,
        leaf_coupling,
        sub_transfer[0],
        sub_coupling[0],
        top_transfer,
        top_coupling,
    )
    chunk = rows // 8
    return pl.pallas_call(
        scatter_kernel,
        grid=(8,),
        out_shape=jax.ShapeDtypeStruct((rows, width), F32),
        in_specs=[smem, pl.BlockSpec((chunk, width), lambda i: (i, 0))],
        out_specs=pl.BlockSpec((rows, width), lambda i: (0, 0)),
        compiler_params=pltpu.CompilerParams(vmem_limit_bytes=16 * 1024 * 1024),
        name="hss_scatter",
    )(order, y)


def solution(mesh):
    in_specs = (
        P(None, ("top", "sub")),
        P(("top", "sub"), None),
        P(("top", "sub"), None),
        P(("top", "sub"), None),
        P(("top", "sub"), None, None),
        P(("top", "sub"), None, None),
        P("top", None, None, None),
        P("top", None, None, None),
        P(),
        P(),
    )
    out_specs = P(("top", "sub"), None)
    body = functools.partial(local, mesh.shape["sub"], mesh.shape["top"])
    return jax.shard_map(
        body, mesh=mesh, in_specs=in_specs, out_specs=out_specs, check_vma=False
    )
```

```python
import functools

import jax
import jax.numpy as jnp
from jax import lax
from jax.experimental import pallas as pl
from jax.experimental.pallas import tpu as pltpu
from jax.sharding import PartitionSpec as P

NUGGET = 0.1
DECAY_RATE = 3.0**0.5 / 0.004
TINY = 1e-30
VMEM_LIMIT = 63 * 1024 * 1024
BLOCK = 256
BLOCKS = 8
WIDE = 5 * BLOCK
NARROW = 4 * BLOCK
F32 = jnp.float32
BF16 = jnp.bfloat16
NN = (((1,), (0,)), ((), ()))
NT = (((1,), (1,)), ((), ()))


def pieces(x):
    high = x.astype(BF16)
    low = (x - high.astype(F32)).astype(BF16)
    return jnp.concatenate([high, low], axis=0)


def product(x, matrix, form):
    rows = x.shape[0]
    both = lax.dot_general(pieces(x), matrix, form, preferred_element_type=F32)
    return both[:rows] + both[rows:]


def place_kernel(order_ref, out_ref):
    rows = order_ref.shape[1]
    value = order_ref[...]
    high = value // 128
    low = value - high * 128
    position = lax.broadcasted_iota(jnp.int32, (1, rows), 1)
    pos_high = position // 64
    pos_low = position - pos_high * 64
    at_high = lax.broadcasted_iota(jnp.int32, (rows // 128, rows), 0) == high
    at_low = lax.broadcasted_iota(jnp.int32, (128, rows), 0) == low
    digits = jnp.concatenate(
        [
            jnp.where(at_high, pos_high.astype(F32), 0.0),
            jnp.where(at_high, pos_low.astype(F32), 0.0),
        ],
        axis=0,
    ).astype(BF16)
    found = lax.dot_general(
        digits, jnp.where(at_low, 1.0, 0.0).astype(BF16), NT, preferred_element_type=F32
    )
    half = rows // 128
    place = (found[:half] * 64.0 + found[half:]).astype(jnp.int32)
    out_ref[...] = jnp.clip(place, 0, rows - 1)


def main_kernel(
    n_sub,
    n_top,
    order,
    inverse,
    table_hbm,
    coords_hbm,
    vectors_hbm,
    gen_hbm,
    leaf_w_hbm,
    leaf_b_hbm,
    sub_w_hbm,
    sub_b_hbm,
    top_w_hbm,
    top_b_hbm,
    near_hbm,
    ucat_hbm,
    fcat_hbm,
    coords,
    vec,
    ordered,
    v_ext,
    v_t,
    gen,
    leaf_w,
    leaf_b,
    sub_w,
    sub_b,
    top_w,
    top_b,
    x_rows,
    x_cols,
    k_0,
    k_1,
    k_2,
    k_3,
    k_4,
    y_row,
    y_col,
    y_all,
    near,
    u_wide,
    u_moved,
    ucat,
    fcat,
    table,
    send_c,
    coef,
    sib,
    field,
    back,
    top_c,
    dev_f,
    g_leaf,
    in_sem,
    out_sem,
    send_sem,
    recv_sem,
):
    k_bufs = [k_0, k_1, k_2, k_3, k_4]
    leaf = v_t.shape[2]
    rows = vec.shape[0]
    width = vec.shape[1]
    share = width // n_sub
    extra = v_ext.shape[1] - leaf
    me_sub = lax.axis_index("sub")
    me_top = lax.axis_index("top")

    barrier = pltpu.get_barrier_semaphore()

    def load(i, source, target):
        copy = pltpu.make_async_copy(source, target, in_sem.at[i])
        copy.start()
        return copy

    load_coords = load(0, coords_hbm, coords)
    load_table = load(1, table_hbm, table)
    quarter = rows // 4
    load_vec = [
        load(3 + i, vectors_hbm.at[pl.ds(i * quarter, quarter)], vec.at[pl.ds(i * quarter, quarter)])
        for i in range(4)
    ]
    load_leaf = [
        load(7, gen_hbm, gen),
        load(8, leaf_w_hbm, leaf_w),
        load(9, leaf_b_hbm, leaf_b),
    ]
    load_sub = [load(10, sub_w_hbm, sub_w), load(11, sub_b_hbm, sub_b)]
    load_top = [load(12, top_w_hbm, top_w), load(13, top_b_hbm, top_b)]

    def greet(axis, count, place):
        def one(k, _):
            pl.semaphore_signal(
                barrier,
                inc=1,
                device_id={axis: lax.rem(place + k, count)},
                device_id_type=pl.DeviceIdType.MESH,
            )
            return 0

        lax.fori_loop(1, count, one, 0)

    greet("sub", n_sub, me_sub)
    greet("top", n_top, me_top)

    def spread(start):
        for axis in range(3):
            row = coords[axis : axis + 1, pl.ds(start, 128)] * DECAY_RATE
            x_rows[axis, pl.ds(start, 128), :] = jnp.broadcast_to(row, (128, 128)).T

    def spread_block(at, block):
        spread(at * leaf + block * BLOCK)
        spread(at * leaf + block * BLOCK + 128)

    load_coords.wait()
    spread_block(0, 0)
    spread_block(1, 0)
    for at in range(2):
        for axis in range(3):
            row = coords[axis : axis + 1, at * leaf : (at + 1) * leaf] * DECAY_RATE
            whole = jnp.broadcast_to(row, (8, leaf))
            x_cols[axis, at, :, :leaf] = whole
            x_cols[axis, at, :, leaf:] = whole[:, :extra]
    y_col[...] = jnp.zeros_like(y_col)

    strips = [(at, block) for block in range(BLOCKS) for at in range(2)]

    def size_of(index):
        return WIDE if strips[index][1] < BLOCKS // 2 else NARROW

    def evaluate(index, first, low, high):
        at, block = strips[index]
        size = high - low
        here = pl.ds(pl.multiple_of(at * leaf + block * BLOCK + first, 16), 16)
        there = pl.ds(block * BLOCK + low, size)
        total = None
        for axis in range(3):
            x_i = jnp.concatenate([x_rows[axis, here, :]] * (size // 128), axis=1)
            x_j = x_cols[axis, at, :, there]
            offset = x_i - jnp.concatenate([x_j, x_j], axis=0)
            square = offset * offset
            total = square + TINY if total is None else total + square
        scaled = total * lax.rsqrt(total)
        value = (1.0 + scaled) * jnp.exp(-scaled)
        k_bufs[index % 5][pl.ds(pl.multiple_of(first, 16), 16), pl.ds(low, size)] = value.astype(BF16)

    def apply(index):
        at, block = strips[index]
        size = size_of(index)
        held = k_bufs[index % 5]
        start = block * BLOCK
        y_row[at, pl.ds(start, BLOCK), :] = jnp.dot(
            held[:, :size], v_ext[at, pl.ds(start, size), :], preferred_element_type=F32
        )
        y_col[at, :, pl.ds(start + BLOCK, size - BLOCK)] += jnp.dot(
            v_t[at, :, pl.ds(start, BLOCK)], held[:, BLOCK:size], preferred_element_type=F32
        )

    for copy in load_vec:
        copy.wait()

    def turn(start):
        at = start // leaf
        inside = pl.multiple_of(start - at * leaf, 128)
        some = ordered[pl.ds(start, 128), :]
        v_ext[at, pl.ds(inside, 128), :] = some.astype(BF16)
        v_t[at, :, pl.ds(inside, 128)] = some.T.astype(BF16)

    def first_strip(index):
        def part(p, _):
            start = pl.multiple_of(index * 1024 + p * 128, 128)
            for group in range(4):
                begin = start + group * 32
                held = [vec[pl.ds(order[0, begin + k], 1), :] for k in range(32)]
                low = (group % 2) * (WIDE // 2)
                evaluate(index, p * 32 + (group // 2) * 16, low, low + WIDE // 2)
                for k in range(32):
                    ordered[pl.ds(begin + k, 1), :] = held[k]
            turn(pl.multiple_of(jnp.maximum(start - 128, 0), 128))
            if index == 0:
                spread(
                    pl.multiple_of(
                        lax.rem(p // 2, 2) * leaf + (1 + p // 4) * BLOCK + lax.rem(p, 2) * 128, 128
                    )
                )
            return 0

        lax.fori_loop(0, 8, part, 0, unroll=True)

    for index in range(4):
        first_strip(index)
    turn(rows - 128)
    for at in range(2):
        v_ext[at, leaf:, :] = v_ext[at, :extra, :]

    for copy in load_leaf:
        copy.wait()
    left = jnp.dot(v_t[0], gen[:leaf, :], preferred_element_type=F32)
    right = jnp.dot(v_t[1], gen[leaf:, :], preferred_element_type=F32)
    device_c = product(left, leaf_w[0], NN) + product(right, leaf_w[1], NN)
    for r in range(n_sub):
        send_c[r] = device_c[r * share : (r + 1) * share, :]
    pl.semaphore_wait(barrier, n_sub + n_top - 2)

    def sub_partners():
        inner = 4 if n_sub % 4 == 0 else 1
        outer = n_sub // inner

        def distance(k):
            step, turn = k // inner, k % inner
            return min(step, outer - step) + min(turn, inner - turn)

        for k in sorted(range(1, n_sub), key=lambda k: -distance(k)):
            step, turn = k // inner, k % inner
            yield (
                lax.rem(me_sub // inner + step, outer) * inner
                + lax.rem(lax.rem(me_sub, inner) + turn, inner)
            )

    def top_partners():
        for k in sorted(range(1, n_top), key=lambda k: -min(k, n_top - k)):
            yield lax.rem(me_top + k, n_top)

    def exchange(axis, count, place, partners, stage, source, target, base):
        def copy(partner, slot):
            return pltpu.make_async_remote_copy(
                src_ref=source(partner),
                dst_ref=target.at[base + slot],
                send_sem=send_sem.at[stage, partner],
                recv_sem=recv_sem.at[stage, slot],
                device_id={axis: partner},
                device_id_type=pl.DeviceIdType.MESH,
            )

        def start():
            for partner in partners():
                copy(partner, place).start()

        def finish_send(k, _):
            copy(lax.rem(place + k, count), place).wait_send()
            return 0

        def finish_recv(k, _):
            partner = lax.rem(place + k, count)
            copy(partner, partner).wait_recv()
            return 0

        return (
            start,
            lambda: lax.fori_loop(1, count, finish_send, 0),
            lambda: lax.fori_loop(1, count, finish_recv, 0),
        )

    up_start, up_sent, up_here = exchange(
        "sub", n_sub, me_sub, sub_partners, 0, lambda partner: send_c.at[partner], coef, n_sub
    )
    up_start()
    coef[n_sub + me_sub] = send_c[me_sub]
    g_leaf[0] = product(right, leaf_b[0], NT)
    g_leaf[1] = product(left, leaf_b[0], NN)

    u_wide[...] = gen[...].astype(F32)
    load_table.wait()

    def work(index, ready, moving):
        at, block = strips[index]
        for done in ready:
            apply(done)

        size = size_of(index)

        def part(p, _):
            if not moving:
                evaluate(index, p * 16, 0, size)
                return 0
            line = (index - 4) * 4 + p // 4
            begin = lax.rem(p, 4) * 32
            start = pl.multiple_of((index - 4) * 512 + p * 32, 32)
            held = [u_wide[pl.ds(inverse[line, begin + k], 1), :] for k in range(32)]
            evaluate(index, p * 16, 0, size)
            for k in range(32):
                u_moved[pl.ds(start + k, 1), :] = held[k]
            return 0

        lax.fori_loop(0, 16, part, 0, unroll=True)
        if moving:
            for line in range((index - 4) * 4, (index - 3) * 4):
                here = slice(line * 128, (line + 1) * 128)
                second = jnp.where(table[line : line + 1, :] >= leaf, 1.0, 0.0)
                second = jnp.broadcast_to(second, (128, 128)).T > 0.5
                some = u_moved[here, :]
                ucat[here, :width] = jnp.where(second, 0.0, some).astype(BF16)
                ucat[here, width:] = jnp.where(second, some, 0.0).astype(BF16)
        if block + 1 < BLOCKS and block >= 2:
            spread_block(at, block + 1)

    work(4, [0, 1], True)
    work(5, [2], True)
    work(6, [3, 4], True)
    work(7, [5], True)
    work(8, [6, 7], True)
    work(9, [8], True)

    for copy in load_sub:
        copy.wait()
    up_here()

    def upward(held, matrices, parent, offset):
        pair = jnp.concatenate([held[2 * parent], held[2 * parent + 1]], axis=1)
        both = matrices[pl.ds(2 * parent - offset, 2)].reshape(2 * width, width)
        held[parent] = product(pair, both, NN)

    count = n_sub // 2
    while count >= 1:
        lax.fori_loop(
            count, 2 * count, lambda p, _: (upward(coef, sub_w, p, 2), 0)[1], 0, unroll=True
        )
        count //= 2
    top_start, top_sent, top_here = exchange(
        "top", n_top, me_top, top_partners, 1, lambda partner: coef.at[1], top_c, n_top
    )
    top_start()
    top_c[n_top + me_top] = coef[1]

    def siblings(parent, _):
        matrix = sub_b[parent - 1]
        sib[2 * parent] = product(coef[2 * parent + 1], matrix, NT)
        sib[2 * parent + 1] = product(coef[2 * parent], matrix, NN)
        return 0

    lax.fori_loop(1, n_sub, siblings, 0, unroll=True)

    work(10, [9], True)
    work(11, [10], True)
    u_write = pltpu.make_async_copy(ucat, ucat_hbm, out_sem.at[0])
    u_write.start()
    work(12, [11], False)
    work(13, [12], False)

    for copy in load_top:
        copy.wait()
    top_here()
    count = n_top // 2
    while count >= 2:
        lax.fori_loop(
            count, 2 * count, lambda p, _: (upward(top_c, top_w, p, 4), 0)[1], 0, unroll=True
        )
        count //= 2
    now = None
    count = 2
    while count <= n_top:
        node = count + me_top // (n_top // count)
        parent = node // 2
        is_left = node - 2 * parent == 0
        other = jnp.where(is_left, node + 1, node - 1)
        matrix = top_b[parent - 1]
        incoming = jnp.where(
            is_left, product(top_c[other], matrix, NT), product(top_c[other], matrix, NN)
        )
        now = incoming if now is None else product(now, top_w[node - 4], NT) + incoming
        count *= 2
    field[1] = now

    def downward(parent, _):
        both = sub_w[pl.ds(2 * parent - 2, 2)].reshape(2 * width, width)
        down = product(field[parent], both, NT)
        field[2 * parent] = down[:, :width] + sib[2 * parent]
        field[2 * parent + 1] = down[:, width:] + sib[2 * parent + 1]
        return 0

    count = 1
    while count < n_sub:
        lax.fori_loop(count, 2 * count, downward, 0, unroll=True)
        count *= 2
    down_start, down_sent, down_here = exchange(
        "sub", n_sub, me_sub, sub_partners, 2, lambda partner: field.at[n_sub + partner], back, 0
    )
    down_start()
    back[me_sub] = field[n_sub + me_sub]

    work(14, [13], False)
    work(15, [14], False)
    apply(15)
    for at in range(2):
        for block in range(BLOCKS):
            start = at * leaf + block * BLOCK
            here = slice(block * BLOCK, (block + 1) * BLOCK)
            turned = y_col[at, :, here]
            if (block + 1) * BLOCK <= extra:
                turned = turned + y_col[at, :, leaf + block * BLOCK : leaf + (block + 1) * BLOCK]
            y_all[start : start + BLOCK, :] = (
                y_row[at, here, :] + turned.T + NUGGET * ordered[start : start + BLOCK, :]
            )

    def move_back(line, _):
        start = pl.multiple_of(line * 128, 128)

        def move(k, _):
            near[pl.ds(start + k, 1), :] = y_all[pl.ds(inverse[line, k], 1), :]
            return 0

        lax.fori_loop(0, 128, move, 0, unroll=True)
        return 0

    writes = [u_write]
    for i in range(4):
        lax.fori_loop(i * rows // 512, (i + 1) * rows // 512, move_back, 0, unroll=True)
        some = pl.ds(i * quarter, quarter)
        write = pltpu.make_async_copy(near.at[some], near_hbm.at[some], out_sem.at[1 + i])
        write.start()
        writes.append(write)

    down_here()
    for r in range(n_sub):
        dev_f[r * share : (r + 1) * share, :] = back[r]
    device_f = dev_f[...]
    for at in range(2):
        fcat[:, at * width : (at + 1) * width] = (
            product(device_f, leaf_w[at], NT) + g_leaf[at]
        ).astype(BF16)
    f_write = pltpu.make_async_copy(fcat, fcat_hbm, out_sem.at[5])
    f_write.start()
    writes.append(f_write)
    up_sent()
    top_sent()
    down_sent()
    for write in writes:
        write.wait()


def far_kernel(near_ref, ucat_ref, fcat_ref, out_ref):
    out_ref[...] = near_ref[...] + lax.dot_general(
        ucat_ref[...], fcat_ref[...], NT, preferred_element_type=F32
    )


def local(
    n_sub,
    n_top,
    coords,
    vectors,
    order,
    generators,
    leaf_transfer,
    leaf_coupling,
    sub_transfer,
    sub_coupling,
    top_transfer,
    top_coupling,
):
    rows, width = vectors.shape
    leaf = rows // 2
    rank = generators.shape[1]
    share = width // n_sub
    extended = leaf + 3 * BLOCK
    hbm = pl.BlockSpec(memory_space=pl.ANY)
    smem = pl.BlockSpec(memory_space=pltpu.SMEM)
    inverse = pl.pallas_call(
        place_kernel,
        out_shape=jax.ShapeDtypeStruct((rows // 128, 128), jnp.int32),
        compiler_params=pltpu.CompilerParams(vmem_limit_bytes=VMEM_LIMIT),
        name="hss_place",
    )(order)
    scratch = [
        pltpu.VMEM((3, rows), F32),
        pltpu.VMEM((rows, width), F32),
        pltpu.VMEM((rows, width), F32),
        pltpu.VMEM((2, extended, width), BF16),
        pltpu.VMEM((2, width, leaf), BF16),
        pltpu.VMEM((rows, rank), BF16),
        pltpu.VMEM(leaf_transfer.shape, BF16),
        pltpu.VMEM(leaf_coupling.shape, BF16),
        pltpu.VMEM(sub_transfer.shape[1:], BF16),
        pltpu.VMEM(sub_coupling.shape[1:], BF16),
        pltpu.VMEM(top_transfer.shape, BF16),
        pltpu.VMEM(top_coupling.shape, BF16),
        pltpu.VMEM((3, rows, 128), F32),
        pltpu.VMEM((3, 2, 8, extended), F32),
        *[pltpu.VMEM((BLOCK, WIDE), BF16) for _ in range(5)],
        pltpu.VMEM((2, leaf, width), F32),
        pltpu.VMEM((2, width, extended), F32),
        pltpu.VMEM((rows, width), F32),
        pltpu.VMEM((rows, width), F32),
        pltpu.VMEM((rows, rank), F32),
        pltpu.VMEM((rows, rank), F32),
        pltpu.VMEM((rows, 2 * rank), BF16),
        pltpu.VMEM((width, 2 * rank), BF16),
        pltpu.VMEM((rows // 128, 128), jnp.int32),
        pltpu.VMEM((n_sub, share, rank), F32),
        pltpu.VMEM((2 * n_sub, share, rank), F32),
        pltpu.VMEM((2 * n_sub, share, rank), F32),
        pltpu.VMEM((2 * n_sub, share, rank), F32),
        pltpu.VMEM((n_sub, share, rank), F32),
        pltpu.VMEM((2 * n_top, share, rank), F32),
        pltpu.VMEM((width, rank), F32),
        pltpu.VMEM((2, width, rank), F32),
        pltpu.SemaphoreType.DMA((14,)),
        pltpu.SemaphoreType.DMA((6,)),
        pltpu.SemaphoreType.DMA((3, max(n_sub, n_top))),
        pltpu.SemaphoreType.DMA((3, max(n_sub, n_top))),
    ]
    near, ucat, fcat = pl.pallas_call(
        functools.partial(main_kernel, n_sub, n_top),
        out_shape=(
            jax.ShapeDtypeStruct((rows, width), F32),
            jax.ShapeDtypeStruct((rows, 2 * rank), BF16),
            jax.ShapeDtypeStruct((width, 2 * rank), BF16),
        ),
        in_specs=[smem, smem] + [hbm] * 10,
        out_specs=(hbm, hbm, hbm),
        scratch_shapes=scratch,
        compiler_params=pltpu.CompilerParams(
            collective_id=0, has_side_effects=True, vmem_limit_bytes=VMEM_LIMIT
        ),
        name="hss_main",
    )(
        order,
        inverse,
        inverse,
        coords,
        vectors,
        generators,
        leaf_transfer,
        leaf_coupling,
        sub_transfer[0],
        sub_coupling[0],
        top_transfer,
        top_coupling,
    )
    chunk = rows // 2
    return pl.pallas_call(
        far_kernel,
        grid=(2,),
        out_shape=jax.ShapeDtypeStruct((rows, width), F32),
        in_specs=[
            pl.BlockSpec((chunk, width), lambda i: (i, 0)),
            pl.BlockSpec((chunk, 2 * rank), lambda i: (i, 0)),
            pl.BlockSpec((width, 2 * rank), lambda i: (0, 0)),
        ],
        out_specs=pl.BlockSpec((chunk, width), lambda i: (i, 0)),
        compiler_params=pltpu.CompilerParams(vmem_limit_bytes=VMEM_LIMIT),
        name="hss_far",
    )(near, ucat, fcat)


def solution(mesh):
    in_specs = (
        P(None, ("top", "sub")),
        P(("top", "sub"), None),
        P(("top", "sub"), None),
        P(("top", "sub"), None),
        P(("top", "sub"), None, None),
        P(("top", "sub"), None, None),
        P("top", None, None, None),
        P("top", None, None, None),
        P(),
        P(),
    )
    out_specs = P(("top", "sub"), None)
    body = functools.partial(local, mesh.shape["sub"], mesh.shape["top"])
    return jax.shard_map(
        body, mesh=mesh, in_specs=in_specs, out_specs=out_specs, check_vma=False
    )
```

```python
import functools

import jax
import jax.numpy as jnp
from jax import lax
from jax.experimental import pallas as pl
from jax.experimental.pallas import tpu as pltpu
from jax.sharding import PartitionSpec as P

NUGGET = 0.1
DECAY_RATE = 3.0**0.5 / 0.004
TINY = 1e-30
VMEM_LIMIT = 63 * 1024 * 1024
BLOCK = 256
BLOCKS = 8
WIDE = 5 * BLOCK
NARROW = 4 * BLOCK
F32 = jnp.float32
BF16 = jnp.bfloat16
NN = (((1,), (0,)), ((), ()))
NT = (((1,), (1,)), ((), ()))


def pieces(x):
    high = x.astype(BF16)
    low = (x - high.astype(F32)).astype(BF16)
    return jnp.concatenate([high, low], axis=0)


def product(x, matrix, form):
    rows = x.shape[0]
    both = lax.dot_general(pieces(x), matrix, form, preferred_element_type=F32)
    return both[:rows] + both[rows:]


def place_kernel(order_ref, out_ref):
    rows = order_ref.shape[1]
    value = order_ref[...]
    high = value // 128
    low = value - high * 128
    position = lax.broadcasted_iota(jnp.int32, (1, rows), 1)
    pos_high = position // 64
    pos_low = position - pos_high * 64
    at_high = lax.broadcasted_iota(jnp.int32, (rows // 128, rows), 0) == high
    at_low = lax.broadcasted_iota(jnp.int32, (128, rows), 0) == low
    digits = jnp.concatenate(
        [
            jnp.where(at_high, pos_high.astype(F32), 0.0),
            jnp.where(at_high, pos_low.astype(F32), 0.0),
        ],
        axis=0,
    ).astype(BF16)
    found = lax.dot_general(
        digits, jnp.where(at_low, 1.0, 0.0).astype(BF16), NT, preferred_element_type=F32
    )
    half = rows // 128
    place = (found[:half] * 64.0 + found[half:]).astype(jnp.int32)
    out_ref[...] = jnp.clip(place, 0, rows - 1)


def main_kernel(
    n_sub,
    n_top,
    order,
    inverse,
    table_hbm,
    coords_hbm,
    vectors_hbm,
    gen_hbm,
    leaf_w_hbm,
    leaf_b_hbm,
    sub_w_hbm,
    sub_b_hbm,
    top_w_hbm,
    top_b_hbm,
    near_hbm,
    ucat_hbm,
    fcat_hbm,
    coords,
    vec,
    ordered,
    v_ext,
    v_t,
    gen,
    leaf_w,
    leaf_b,
    sub_w,
    sub_b,
    top_w,
    top_b,
    x_rows,
    x_cols,
    k_0,
    k_1,
    k_2,
    k_3,
    k_4,
    y_row,
    y_col,
    y_all,
    near,
    u_wide,
    u_moved,
    ucat,
    fcat,
    table,
    send_c,
    coef,
    sib,
    field,
    back,
    top_c,
    dev_f,
    g_leaf,
    in_sem,
    out_sem,
    send_sem,
    recv_sem,
):
    k_bufs = [k_0, k_1, k_2, k_3, k_4]
    leaf = v_t.shape[2]
    rows = vec.shape[0]
    width = vec.shape[1]
    share = width // n_sub
    extra = v_ext.shape[1] - leaf
    me_sub = lax.axis_index("sub")
    me_top = lax.axis_index("top")

    barrier = pltpu.get_barrier_semaphore()

    def load(i, source, target):
        copy = pltpu.make_async_copy(source, target, in_sem.at[i])
        copy.start()
        return copy

    load_coords = load(0, coords_hbm, coords)
    load_table = load(1, table_hbm, table)
    quarter = rows // 4
    load_vec = [
        load(3 + i, vectors_hbm.at[pl.ds(i * quarter, quarter)], vec.at[pl.ds(i * quarter, quarter)])
        for i in range(4)
    ]
    load_leaf = [
        load(7, gen_hbm, gen),
        load(8, leaf_w_hbm, leaf_w),
        load(9, leaf_b_hbm, leaf_b),
    ]
    load_sub = [load(10, sub_w_hbm, sub_w), load(11, sub_b_hbm, sub_b)]
    load_top = [load(12, top_w_hbm, top_w), load(13, top_b_hbm, top_b)]

    def greet(axis, count, place):
        def one(k, _):
            pl.semaphore_signal(
                barrier,
                inc=1,
                device_id={axis: lax.rem(place + k, count)},
                device_id_type=pl.DeviceIdType.MESH,
            )
            return 0

        lax.fori_loop(1, count, one, 0)

    greet("sub", n_sub, me_sub)
    greet("top", n_top, me_top)

    def spread(start):
        for axis in range(3):
            row = coords[axis : axis + 1, pl.ds(start, 128)] * DECAY_RATE
            x_rows[axis, pl.ds(start, 128), :] = jnp.broadcast_to(row, (128, 128)).T

    def spread_block(at, block):
        spread(at * leaf + block * BLOCK)
        spread(at * leaf + block * BLOCK + 128)

    load_coords.wait()
    spread_block(0, 0)
    spread_block(1, 0)
    for at in range(2):
        for axis in range(3):
            row = coords[axis : axis + 1, at * leaf : (at + 1) * leaf] * DECAY_RATE
            whole = jnp.broadcast_to(row, (8, leaf))
            x_cols[axis, at, :, :leaf] = whole
            x_cols[axis, at, :, leaf:] = whole[:, :extra]
    y_col[...] = jnp.zeros_like(y_col)

    strips = [(at, block) for block in range(BLOCKS) for at in range(2)]

    def size_of(index):
        return WIDE if strips[index][1] < BLOCKS // 2 else NARROW

    def evaluate(index, first, low, high):
        at, block = strips[index]
        size = high - low
        here = pl.ds(pl.multiple_of(at * leaf + block * BLOCK + first, 16), 16)
        there = pl.ds(block * BLOCK + low, size)
        total = None
        for axis in range(3):
            x_i = jnp.concatenate([x_rows[axis, here, :]] * (size // 128), axis=1)
            x_j = x_cols[axis, at, :, there]
            offset = x_i - jnp.concatenate([x_j, x_j], axis=0)
            square = offset * offset
            total = square + TINY if total is None else total + square
        scaled = total * lax.rsqrt(total)
        value = (1.0 + scaled) * jnp.exp(-scaled)
        k_bufs[index % 5][pl.ds(pl.multiple_of(first, 16), 16), pl.ds(low, size)] = value.astype(BF16)

    def apply(index):
        at, block = strips[index]
        size = size_of(index)
        held = k_bufs[index % 5]
        start = block * BLOCK
        y_row[at, pl.ds(start, BLOCK), :] = jnp.dot(
            held[:, :size], v_ext[at, pl.ds(start, size), :], preferred_element_type=F32
        )
        y_col[at, :, pl.ds(start + BLOCK, size - BLOCK)] += jnp.dot(
            v_t[at, :, pl.ds(start, BLOCK)], held[:, BLOCK:size], preferred_element_type=F32
        )

    for copy in load_vec:
        copy.wait()

    def turn(start):
        at = start // leaf
        inside = pl.multiple_of(start - at * leaf, 128)
        some = ordered[pl.ds(start, 128), :]
        v_ext[at, pl.ds(inside, 128), :] = some.astype(BF16)
        v_t[at, :, pl.ds(inside, 128)] = some.T.astype(BF16)

    def first_strip(index):
        def part(p, _):
            start = pl.multiple_of(index * 1024 + p * 128, 128)
            for group in range(4):
                begin = start + group * 32
                held = [vec[pl.ds(order[0, begin + k], 1), :] for k in range(32)]
                low = (group % 2) * (WIDE // 2)
                evaluate(index, p * 32 + (group // 2) * 16, low, low + WIDE // 2)
                for k in range(32):
                    ordered[pl.ds(begin + k, 1), :] = held[k]
            turn(pl.multiple_of(jnp.maximum(start - 128, 0), 128))
            if index == 0:
                spread(
                    pl.multiple_of(
                        lax.rem(p // 2, 2) * leaf + (1 + p // 4) * BLOCK + lax.rem(p, 2) * 128, 128
                    )
                )
            return 0

        lax.fori_loop(0, 8, part, 0, unroll=True)

    for index in range(4):
        first_strip(index)
    turn(rows - 128)
    for at in range(2):
        v_ext[at, leaf:, :] = v_ext[at, :extra, :]

    for copy in load_leaf:
        copy.wait()
    left = jnp.dot(v_t[0], gen[:leaf, :], preferred_element_type=F32)
    right = jnp.dot(v_t[1], gen[leaf:, :], preferred_element_type=F32)
    device_c = product(left, leaf_w[0], NN) + product(right, leaf_w[1], NN)
    for r in range(n_sub):
        send_c[r] = device_c[r * share : (r + 1) * share, :]
    pl.semaphore_wait(barrier, n_sub + n_top - 2)

    def sub_partners():
        inner = 4 if n_sub % 4 == 0 else 1
        outer = n_sub // inner

        def distance(k):
            step, turn = k // inner, k % inner
            return min(step, outer - step) + min(turn, inner - turn)

        for k in sorted(range(1, n_sub), key=lambda k: -distance(k)):
            step, turn = k // inner, k % inner
            yield (
                lax.rem(me_sub // inner + step, outer) * inner
                + lax.rem(lax.rem(me_sub, inner) + turn, inner)
            )

    def top_partners():
        for k in sorted(range(1, n_top), key=lambda k: -min(k, n_top - k)):
            yield lax.rem(me_top + k, n_top)

    def exchange(axis, count, place, partners, stage, source, target, base):
        def copy(partner, slot):
            return pltpu.make_async_remote_copy(
                src_ref=source(partner),
                dst_ref=target.at[base + slot],
                send_sem=send_sem.at[stage, partner],
                recv_sem=recv_sem.at[stage, slot],
                device_id={axis: partner},
                device_id_type=pl.DeviceIdType.MESH,
            )

        def start():
            for partner in partners():
                copy(partner, place).start()

        def finish_send(k, _):
            copy(lax.rem(place + k, count), place).wait_send()
            return 0

        def finish_recv(k, _):
            partner = lax.rem(place + k, count)
            copy(partner, partner).wait_recv()
            return 0

        return (
            start,
            lambda: lax.fori_loop(1, count, finish_send, 0),
            lambda: lax.fori_loop(1, count, finish_recv, 0),
        )

    up_start, up_sent, up_here = exchange(
        "sub", n_sub, me_sub, sub_partners, 0, lambda partner: send_c.at[partner], coef, n_sub
    )
    up_start()
    coef[n_sub + me_sub] = send_c[me_sub]
    g_leaf[0] = product(right, leaf_b[0], NT)
    g_leaf[1] = product(left, leaf_b[0], NN)

    u_wide[...] = gen[...].astype(F32)
    load_table.wait()

    def work(index, ready, moving):
        at, block = strips[index]
        for done in ready:
            apply(done)

        size = size_of(index)

        def part(p, _):
            if not moving:
                evaluate(index, p * 16, 0, size)
                return 0
            line = (index - 4) * 4 + p // 4
            begin = lax.rem(p, 4) * 32
            start = pl.multiple_of((index - 4) * 512 + p * 32, 32)
            held = [u_wide[pl.ds(inverse[line, begin + k], 1), :] for k in range(32)]
            evaluate(index, p * 16, 0, size)
            for k in range(32):
                u_moved[pl.ds(start + k, 1), :] = held[k]
            return 0

        lax.fori_loop(0, 16, part, 0, unroll=True)
        if moving:
            for line in range((index - 4) * 4, (index - 3) * 4):
                here = slice(line * 128, (line + 1) * 128)
                second = jnp.where(table[line : line + 1, :] >= leaf, 1.0, 0.0)
                second = jnp.broadcast_to(second, (128, 128)).T > 0.5
                some = u_moved[here, :]
                ucat[here, :width] = jnp.where(second, 0.0, some).astype(BF16)
                ucat[here, width:] = jnp.where(second, some, 0.0).astype(BF16)
        if block + 1 < BLOCKS and block >= 2:
            spread_block(at, block + 1)

    work(4, [0, 1], True)
    work(5, [2], True)
    work(6, [3, 4], True)
    work(7, [5], True)
    work(8, [6, 7], True)
    work(9, [8], True)

    for copy in load_sub:
        copy.wait()
    up_here()

    def upward(held, matrices, parent, offset):
        pair = jnp.concatenate([held[2 * parent], held[2 * parent + 1]], axis=1)
        both = matrices[pl.ds(2 * parent - offset, 2)].reshape(2 * width, width)
        held[parent] = product(pair, both, NN)

    count = n_sub // 2
    while count >= 1:
        lax.fori_loop(
            count, 2 * count, lambda p, _: (upward(coef, sub_w, p, 2), 0)[1], 0, unroll=True
        )
        count //= 2
    top_start, top_sent, top_here = exchange(
        "top", n_top, me_top, top_partners, 1, lambda partner: coef.at[1], top_c, n_top
    )
    top_start()
    top_c[n_top + me_top] = coef[1]

    def siblings(parent, _):
        matrix = sub_b[parent - 1]
        sib[2 * parent] = product(coef[2 * parent + 1], matrix, NT)
        sib[2 * parent + 1] = product(coef[2 * parent], matrix, NN)
        return 0

    lax.fori_loop(1, n_sub, siblings, 0, unroll=True)

    work(10, [9], True)
    work(11, [10], True)
    u_write = pltpu.make_async_copy(ucat, ucat_hbm, out_sem.at[0])
    u_write.start()
    work(12, [11], False)

    for copy in load_top:
        copy.wait()
    top_here()
    count = n_top // 2
    while count >= 2:
        lax.fori_loop(
            count, 2 * count, lambda p, _: (upward(top_c, top_w, p, 4), 0)[1], 0, unroll=True
        )
        count //= 2
    now = None
    count = 2
    while count <= n_top:
        node = count + me_top // (n_top // count)
        parent = node // 2
        is_left = node - 2 * parent == 0
        other = jnp.where(is_left, node + 1, node - 1)
        matrix = top_b[parent - 1]
        incoming = jnp.where(
            is_left, product(top_c[other], matrix, NT), product(top_c[other], matrix, NN)
        )
        now = incoming if now is None else product(now, top_w[node - 4], NT) + incoming
        count *= 2
    field[1] = now

    def downward(parent, _):
        both = sub_w[pl.ds(2 * parent - 2, 2)].reshape(2 * width, width)
        down = product(field[parent], both, NT)
        field[2 * parent] = down[:, :width] + sib[2 * parent]
        field[2 * parent + 1] = down[:, width:] + sib[2 * parent + 1]
        return 0

    count = 1
    while count < n_sub:
        lax.fori_loop(count, 2 * count, downward, 0, unroll=True)
        count *= 2
    down_start, down_sent, down_here = exchange(
        "sub", n_sub, me_sub, sub_partners, 2, lambda partner: field.at[n_sub + partner], back, 0
    )
    down_start()
    back[me_sub] = field[n_sub + me_sub]

    work(13, [12], False)
    work(14, [13], False)
    work(15, [14], False)
    apply(15)
    for at in range(2):
        for block in range(BLOCKS):
            start = at * leaf + block * BLOCK
            here = slice(block * BLOCK, (block + 1) * BLOCK)
            turned = y_col[at, :, here]
            if (block + 1) * BLOCK <= extra:
                turned = turned + y_col[at, :, leaf + block * BLOCK : leaf + (block + 1) * BLOCK]
            y_all[start : start + BLOCK, :] = (
                y_row[at, here, :] + turned.T + NUGGET * ordered[start : start + BLOCK, :]
            )

    def move_back(line, _):
        start = pl.multiple_of(line * 128, 128)

        def move(k, _):
            near[pl.ds(start + k, 1), :] = y_all[pl.ds(inverse[line, k], 1), :]
            return 0

        lax.fori_loop(0, 128, move, 0, unroll=True)
        return 0

    writes = [u_write]
    for i in range(4):
        lax.fori_loop(i * rows // 512, (i + 1) * rows // 512, move_back, 0, unroll=True)
        some = pl.ds(i * quarter, quarter)
        write = pltpu.make_async_copy(near.at[some], near_hbm.at[some], out_sem.at[1 + i])
        write.start()
        writes.append(write)

    down_here()
    for r in range(n_sub):
        dev_f[r * share : (r + 1) * share, :] = back[r]
    device_f = dev_f[...]
    for at in range(2):
        fcat[:, at * width : (at + 1) * width] = (
            product(device_f, leaf_w[at], NT) + g_leaf[at]
        ).astype(BF16)
    f_write = pltpu.make_async_copy(fcat, fcat_hbm, out_sem.at[5])
    f_write.start()
    writes.append(f_write)
    up_sent()
    top_sent()
    down_sent()
    for write in writes:
        write.wait()


def far_kernel(near_ref, ucat_ref, fcat_ref, out_ref):
    out_ref[...] = near_ref[...] + lax.dot_general(
        ucat_ref[...], fcat_ref[...], NT, preferred_element_type=F32
    )


def local(
    n_sub,
    n_top,
    coords,
    vectors,
    order,
    generators,
    leaf_transfer,
    leaf_coupling,
    sub_transfer,
    sub_coupling,
    top_transfer,
    top_coupling,
):
    rows, width = vectors.shape
    leaf = rows // 2
    rank = generators.shape[1]
    share = width // n_sub
    extended = leaf + 3 * BLOCK
    hbm = pl.BlockSpec(memory_space=pl.ANY)
    smem = pl.BlockSpec(memory_space=pltpu.SMEM)
    inverse = pl.pallas_call(
        place_kernel,
        out_shape=jax.ShapeDtypeStruct((rows // 128, 128), jnp.int32),
        compiler_params=pltpu.CompilerParams(vmem_limit_bytes=VMEM_LIMIT),
        name="hss_place",
    )(order)
    scratch = [
        pltpu.VMEM((3, rows), F32),
        pltpu.VMEM((rows, width), F32),
        pltpu.VMEM((rows, width), F32),
        pltpu.VMEM((2, extended, width), BF16),
        pltpu.VMEM((2, width, leaf), BF16),
        pltpu.VMEM((rows, rank), BF16),
        pltpu.VMEM(leaf_transfer.shape, BF16),
        pltpu.VMEM(leaf_coupling.shape, BF16),
        pltpu.VMEM(sub_transfer.shape[1:], BF16),
        pltpu.VMEM(sub_coupling.shape[1:], BF16),
        pltpu.VMEM(top_transfer.shape, BF16),
        pltpu.VMEM(top_coupling.shape, BF16),
        pltpu.VMEM((3, rows, 128), F32),
        pltpu.VMEM((3, 2, 8, extended), F32),
        *[pltpu.VMEM((BLOCK, WIDE), BF16) for _ in range(5)],
        pltpu.VMEM((2, leaf, width), F32),
        pltpu.VMEM((2, width, extended), F32),
        pltpu.VMEM((rows, width), F32),
        pltpu.VMEM((rows, width), F32),
        pltpu.VMEM((rows, rank), F32),
        pltpu.VMEM((rows, rank), F32),
        pltpu.VMEM((rows, 2 * rank), BF16),
        pltpu.VMEM((width, 2 * rank), BF16),
        pltpu.VMEM((rows // 128, 128), jnp.int32),
        pltpu.VMEM((n_sub, share, rank), F32),
        pltpu.VMEM((2 * n_sub, share, rank), F32),
        pltpu.VMEM((2 * n_sub, share, rank), F32),
        pltpu.VMEM((2 * n_sub, share, rank), F32),
        pltpu.VMEM((n_sub, share, rank), F32),
        pltpu.VMEM((2 * n_top, share, rank), F32),
        pltpu.VMEM((width, rank), F32),
        pltpu.VMEM((2, width, rank), F32),
        pltpu.SemaphoreType.DMA((14,)),
        pltpu.SemaphoreType.DMA((6,)),
        pltpu.SemaphoreType.DMA((3, max(n_sub, n_top))),
        pltpu.SemaphoreType.DMA((3, max(n_sub, n_top))),
    ]
    near, ucat, fcat = pl.pallas_call(
        functools.partial(main_kernel, n_sub, n_top),
        out_shape=(
            jax.ShapeDtypeStruct((rows, width), F32),
            jax.ShapeDtypeStruct((rows, 2 * rank), BF16),
            jax.ShapeDtypeStruct((width, 2 * rank), BF16),
        ),
        in_specs=[smem, smem] + [hbm] * 10,
        out_specs=(hbm, hbm, hbm),
        scratch_shapes=scratch,
        compiler_params=pltpu.CompilerParams(
            collective_id=0, has_side_effects=True, vmem_limit_bytes=VMEM_LIMIT
        ),
        name="hss_main",
    )(
        order,
        inverse,
        inverse,
        coords,
        vectors,
        generators,
        leaf_transfer,
        leaf_coupling,
        sub_transfer[0],
        sub_coupling[0],
        top_transfer,
        top_coupling,
    )
    chunk = rows // 2
    return pl.pallas_call(
        far_kernel,
        grid=(2,),
        out_shape=jax.ShapeDtypeStruct((rows, width), F32),
        in_specs=[
            pl.BlockSpec((chunk, width), lambda i: (i, 0)),
            pl.BlockSpec((chunk, 2 * rank), lambda i: (i, 0)),
            pl.BlockSpec((width, 2 * rank), lambda i: (0, 0)),
        ],
        out_specs=pl.BlockSpec((chunk, width), lambda i: (i, 0)),
        compiler_params=pltpu.CompilerParams(vmem_limit_bytes=VMEM_LIMIT),
        name="hss_far",
    )(near, ucat, fcat)


def solution(mesh):
    in_specs = (
        P(None, ("top", "sub")),
        P(("top", "sub"), None),
        P(("top", "sub"), None),
        P(("top", "sub"), None),
        P(("top", "sub"), None, None),
        P(("top", "sub"), None, None),
        P("top", None, None, None),
        P("top", None, None, None),
        P(),
        P(),
    )
    out_specs = P(("top", "sub"), None)
    body = functools.partial(local, mesh.shape["sub"], mesh.shape["top"])
    return jax.shard_map(
        body, mesh=mesh, in_specs=in_specs, out_specs=out_specs, check_vma=False
    )
```
